256 devices in a mesh: prow: 32 (over y, x, core), pcol: 8 (over z).
Axes of the slice: x: 4, y: 4, z: 8, core: 2. Of those that a mesh axis runs over, the one named last changes fastest.
Arguments:
- matrix: bfloat16 [1, 32, 256, 8, 8, 256], P(None, 'prow', None, None, 'pcol'), may hold values from -6 to 6
- linv: bfloat16 [3, 256, 256], replicated, may hold values from -0.25 to 1, as said below
- uinv: bfloat16 [3, 256, 256], replicated, may hold values from -0.002 to 0.0079, as said below
Outputs:
- factored: float32 [1, 32, 256, 8, 8, 256], P(None, 'prow', None, None, 'pcol')
The draws below stay inside these ranges and needn't reach their ends.
Inputs may be any that keep to these rules, and one draw needn't show every extreme that they name: linv[k] is unit lower triangular. uinv[k] is upper triangular with a positive diagonal.
All inputs are finite; a program needn't handle non-finite values.
Results may differ from the reference program's by a relative error of at most 0.0017.
Values may be sent and summed in bfloat16 or wider, within the bound.
No kernel may reach another device: no remote copies, remote signals or barrier semaphores. Data moves between devices by JAX's collectives and lax.ppermute only.
A program may use at most 64 MiB of HBM per device.

```python
import jax
import jax.numpy as jnp
from jax import lax

NB = 256
RBD = 1
CBD = 8
PANELS = 3
ROWS = 8192
COLS = 16384
N_PROW = 32
N_PCOL = 8


def triangle_parts(key):
    lower_part = jnp.clip(jax.random.normal(key, (PANELS, NB, NB), jnp.float32) * 0.05, -0.25, 0.25)
    return lower_part


def draw_linv(key, part):
    key = jax.random.fold_in(key, 11)
    lower_part = triangle_parts(key)
    row_iota = lax.broadcasted_iota(jnp.int32, (PANELS, NB, NB), 1)
    col_iota = lax.broadcasted_iota(jnp.int32, (PANELS, NB, NB), 2)
    eye_part = jnp.where(row_iota == col_iota, 1.0, 0.0).astype(jnp.float32)
    return jnp.where(row_iota > col_iota, lower_part, eye_part).astype(jnp.bfloat16)


def draw_uinv(key, part):
    key = jax.random.fold_in(key, 12)
    first_key, second_key = jax.random.split(key)
    upper_part = triangle_parts(first_key)
    scales = jnp.exp(jax.random.uniform(second_key, (PANELS, NB, 1), jnp.float32, jnp.log(1.0 / 512.0), jnp.log(1.0 / 128.0)))
    row_iota = lax.broadcasted_iota(jnp.int32, (PANELS, NB, NB), 1)
    col_iota = lax.broadcasted_iota(jnp.int32, (PANELS, NB, NB), 2)
    eye_part = jnp.where(row_iota == col_iota, 1.0, 0.0).astype(jnp.float32)
    shaped = jnp.where(row_iota < col_iota, upper_part, eye_part)
    return (scales * shaped).astype(jnp.bfloat16)


def level_of(own_key, dims, cuts, least, largest):
    level, own = 1.0, jax.random.fold_in(own_key, 6)
    for dim, parts in cuts:
        draws = jnp.exp(jax.random.uniform(jax.random.fold_in(own, dim), (parts,), jnp.float32, least / len(cuts), largest / len(cuts)))
        level = level * jnp.repeat(draws, dims[dim] // parts).reshape([-1 if axis == dim else 1 for axis in range(len(dims))])
    return level


def bell_draw(rng, dims, scale, reach, cuts=(), kind=jnp.bfloat16):
    drawn = scale * jax.random.normal(rng, dims, jnp.float32)
    if cuts:
        drawn = drawn * level_of(rng, dims, cuts, -0.22, 0.18)
    return jnp.clip(drawn, -reach, reach).astype(kind)


def setup_inputs(seed: int = 0) -> dict:
    streams_of = jax.random.split(jax.random.key(seed), 4)
    matrix = bell_draw(streams_of[0], (RBD, N_PROW, NB, CBD, N_PCOL, NB), 1.0, 6.0, ((1, 32), (4, 8)))
    linv = draw_linv(jax.random.fold_in(streams_of[3], 71), 0)
    uinv = draw_uinv(jax.random.fold_in(streams_of[3], 71), 0)
    return dict(matrix=matrix, linv=linv, uinv=uinv)


def advance(stripe, block_index, step_count, upper_rows, uinv):
    for section in range(step_count):
        done_cols = stripe[:, :section * NB]
        column = stripe[:, section * NB:(section + 1) * NB]
        trailing = stripe[:, (section + 1) * NB:]
        lpanel = jnp.dot(column.astype(jnp.bfloat16), uinv[section], preferred_element_type=jnp.float32).astype(jnp.bfloat16)
        below = block_index > section
        diag_here = block_index == section
        new_col = jnp.where(below, lpanel.astype(jnp.float32), column)
        product = jnp.dot(lpanel, upper_rows[section], preferred_element_type=jnp.float32)
        new_rest = jnp.where(below, trailing - product, jnp.where(diag_here, upper_rows[section].astype(jnp.float32), trailing))
        stripe = jnp.concatenate([done_cols, new_col, new_rest], axis=1)
    return stripe


def reference(matrix, linv, uinv):
    whole_matrix = matrix.reshape(ROWS, COLS)
    upper_rows = []
    for section in range(PANELS):
        stripe = whole_matrix[section * NB:(section + 1) * NB].astype(jnp.float32)
        stripe = advance(stripe, section, section, upper_rows, uinv)
        urow = jnp.dot(linv[section], stripe[:, (section + 1) * NB:].astype(jnp.bfloat16), preferred_element_type=jnp.float32).astype(jnp.bfloat16)
        upper_rows.append(urow)

    def one_block(block_index):
        stripe = lax.dynamic_slice_in_dim(whole_matrix, block_index * NB, NB, 0).astype(jnp.float32)
        return advance(stripe, block_index, PANELS, upper_rows, uinv)

    result = lax.map(one_block, jnp.arange(ROWS // NB, dtype=jnp.int32))
    return result.reshape(matrix.shape)
```

```python
import jax
import jax.numpy as jnp
from jax import lax
from jax.experimental import pallas as pl
from jax.experimental.pallas import tpu as pltpu
from jax.sharding import PartitionSpec as P

BF = jnp.bfloat16
F32 = jnp.float32


def dev(y, x, c):
    return (y % 4) * 8 + (x % 4) * 2 + c


def mm(a, b):
    return jnp.dot(a, b, preferred_element_type=F32)


def zspread(b, z):
    r1 = lax.ppermute(b, "pcol", [(0, 4), (1, 5), (2, 6)])
    h = jnp.where(z >= 4, r1, b)
    r2 = lax.ppermute(h, "pcol", [(0, 2), (2, 0), (1, 3), (4, 6), (6, 4), (5, 7)])
    m = z % 4
    s0 = jnp.where(m < 2, h, r2)
    s1 = jnp.where(m == 0, r2, h)
    r3 = lax.ppermute(jnp.stack([s0, s1]), "pcol", [(i, i ^ 1) for i in range(8)])
    even = m % 2 == 0
    return (
        jnp.where(even, s0, r3[0]),
        jnp.where(even, r3[0], s0),
        jnp.where(even, s1, r3[1]),
    )


def pick(index, options):
    out = options[-1]
    for i in range(len(options) - 2, -1, -1):
        out = jnp.where(index == i, options[i], out)
    return out


def scatter_rows(w, p, t, c):
    hop = lax.ppermute(w[128:], "prow", [(2, 3)])
    v = jnp.where(p == 3, hop, w[:128])
    extra = [(2, 64), (3, 96), (0, 0), (1, 32), None, None]
    got = []
    for j in range(6):
        d, h = 1 + j // 2, j % 2
        pairs = [(0, dev(0, d, 0)), (1, dev(d, 0, 1))]
        value = w[64 * d + 32 * h : 64 * d + 32 * h + 32]
        if extra[j] is not None:
            q, row = extra[j]
            if q != 1:
                pairs.append((2, dev(0, q, 0)))
            pairs.append((3, dev(q, 0, 1)))
            value = jnp.where(p < 2, value, v[row : row + 32])
        got.append(lax.ppermute(value, "prow", pairs))
    first = pick(t, [w[:32], got[0], got[2], got[4]])
    second = pick(t, [w[32:64], got[1], got[3], got[5]])
    third = pick(t, [got[2], jnp.where(c == 0, w[32:64], got[3]), got[0], got[1]])
    return jnp.concatenate([first, second, third])


def broadcast_across(piece, s):
    got = {}
    for d in (2, 1, 3):
        pairs = [(dev(0, k, 0), dev(d, k, 0)) for k in range(4)]
        pairs += [(dev(k, 0, 1), dev(k, d, 1)) for k in range(4)]
        got[d] = lax.ppermute(piece, "prow", pairs)
    return pick(s, [piece, got[1], got[2], got[3]])


def gather_along(piece):
    got = {}
    for d in (2, 1, 3):
        pairs = [(dev(y, x, 0), dev(y, x + d, 0)) for y in range(4) for x in range(4)]
        pairs += [(dev(y, x, 1), dev(y + d, x, 1)) for y in range(4) for x in range(4)]
        got[d] = lax.ppermute(piece, "prow", pairs)
    return jnp.stack([piece, got[1], got[2], got[3]])


def finish_kernel(s_ref, mine, other, w, b, linv, uinv, out, abuf):
    tm, to, c, p, z = (s_ref[i] for i in range(5))

    def assemble(c0, t0, c1, t1):
        for q in range(4):
            j0, j1 = (t0 - q) & 3, (t1 - q) & 3
            abuf[0, 64 * q : 64 * q + 64, :] = c0[j0, 0:64, :]
            abuf[1, 64 * q : 64 * q + 64, :] = c1[j1, 0:64, :]
            abuf[2, 32 * q : 32 * q + 32, :] = c0[j0, 64:96, :]
            abuf[2, 128 + 32 * q : 160 + 32 * q, :] = c1[j1, 64:96, :]

    @pl.when(c == 0)
    def _():
        assemble(mine, tm, other, to)

    @pl.when(c == 1)
    def _():
        assemble(other, to, mine, tm)

    n = w.shape[1]
    c0, c1, c2 = (slice(n + 256 * k, n + 256 * k + 256) for k in range(3))
    u01 = mm(linv[0], abuf[0, :, c1]).astype(BF)
    u02 = mm(linv[0], abuf[0, :, c2]).astype(BF)
    l10 = mm(abuf[1, :, c0], uinv[0]).astype(BF)
    l20 = mm(abuf[2, :, c0], uinv[0]).astype(BF)
    u12 = mm(linv[1], (abuf[1, :, c2].astype(F32) - mm(l10, u02)).astype(BF)).astype(BF)
    l21 = mm((abuf[2, :, c1].astype(F32) - mm(l20, u01)).astype(BF), uinv[1]).astype(BF)
    l0 = mm(b[0], uinv[0]).astype(BF)
    l1 = mm((b[1].astype(F32) - mm(l0, u01)).astype(BF), uinv[1]).astype(BF)
    l2 = mm((b[2].astype(F32) - mm(l0, u02) - mm(l1, u12)).astype(BF), uinv[2]).astype(BF)
    for k in range(n // 256):
        cols = slice(256 * k, 256 * k + 256)
        u0 = mm(linv[0], abuf[0, :, cols]).astype(BF)
        s1 = abuf[1, :, cols].astype(F32) - mm(l10, u0)
        u1 = mm(linv[1], s1.astype(BF)).astype(BF)
        s2 = abuf[2, :, cols].astype(F32) - mm(l20, u0) - mm(l21, u1)
        u2 = mm(linv[2], s2.astype(BF)).astype(BF)
        own = w[:, cols].astype(F32)
        res = own - mm(l0, u0) - mm(l1, u1) - mm(l2, u2)
        res = pick(p, [u0.astype(F32), u1.astype(F32), u2.astype(F32), res])
        if k == 0:
            panel = pick(z, [l0.astype(F32), l1.astype(F32), l2.astype(F32)])
            diag = pick(z, [own, s1, s2])
            special = jnp.where(p > z, panel, jnp.where(p == z, diag, res))
            res = jnp.where(z < 3, special, res)
        out[pl.ds(2 * k, 256, stride=16), :] = res[:, :128]
        out[pl.ds(2 * k + 1, 256, stride=16), :] = res[:, 128:]


def finish(scalars, mine, other, w, b, linv, uinv):
    return pl.pallas_call(
        finish_kernel,
        out_shape=jax.ShapeDtypeStruct((4096, 128), F32),
        in_specs=[pl.BlockSpec(memory_space=pltpu.SMEM)]
        + [pl.BlockSpec(memory_space=pltpu.VMEM)] * 6,
        out_specs=pl.BlockSpec(memory_space=pltpu.VMEM),
        scratch_shapes=[pltpu.VMEM((3, 256, mine.shape[2]), BF)],
        compiler_params=pltpu.CompilerParams(vmem_limit_bytes=40 * 1024 * 1024),
    )(scalars, mine, other, w, b, linv, uinv)


def body(matrix, linv, uinv):
    p, z = lax.axis_index("prow"), lax.axis_index("pcol")
    y, x, c = p // 8, (p // 2) % 4, p % 2
    t = jnp.where(c == 0, x, y)
    s = jnp.where(c == 0, y, x)
    w = matrix.reshape(256, 2048)
    b = jnp.stack(zspread(w[:, :256], z))
    piece = scatter_rows(w, p, t, c)
    corner = zspread(piece[:, :256], z)
    piece = jnp.concatenate([piece, *corner], axis=1)
    piece = broadcast_across(piece, s)
    mine = gather_along(piece)
    other = lax.ppermute(mine, "prow", [(i, i ^ 1) for i in range(32)])
    scalars = jnp.stack([t, s, c, p, z]).astype(jnp.int32)
    out = finish(scalars, mine, other, w, b, linv, uinv)
    return out.reshape(matrix.shape)


def solution(mesh):
    in_specs = (P(None, "prow", None, None, "pcol", None), P(), P())
    out_specs = P(None, "prow", None, None, "pcol", None)
    return jax.shard_map(body, mesh=mesh, in_specs=in_specs, out_specs=out_specs, check_vma=False)
```

```python
import jax
import jax.numpy as jnp
from jax import lax
from jax.experimental import pallas as pl
from jax.experimental.pallas import tpu as pltpu
from jax.sharding import PartitionSpec as P

BF = jnp.bfloat16
F32 = jnp.float32


def dev(y, x, c):
    return (y % 4) * 8 + (x % 4) * 2 + c


def mm(a, b):
    return jnp.dot(a, b, preferred_element_type=F32)


def pick(index, options):
    out = options[-1]
    for i in range(len(options) - 2, -1, -1):
        out = jnp.where(index == i, options[i], out)
    return out


def gather_ring(piece, x_core):
    got = {}
    for d in (2, 1, 3):
        pairs = []
        for y in range(4):
            for x in range(4):
                pairs.append((dev(y, x, x_core), dev(y, x + d, x_core)))
                pairs.append((dev(y, x, 1 - x_core), dev(y + d, x, 1 - x_core)))
        got[d] = lax.ppermute(piece, "prow", pairs)
    return jnp.stack([piece, got[1], got[2], got[3]])


def tie(*arrays):
    return lax.optimization_barrier(arrays)


def z_far(b, z):
    r = lax.ppermute(b, "pcol", [(0, 4), (1, 5), (2, 6)])
    return r


def z_mid(b, z, r1):
    h = jnp.where(z >= 4, r1, b)
    return h, lax.ppermute(h, "pcol", [(0, 2), (2, 0), (1, 3), (4, 6), (6, 4), (5, 7)])


def z_near(z, h, r2):
    m = z % 4
    s0 = jnp.where(m < 2, h, r2)
    s1 = jnp.where(m == 0, r2, h)
    return s0, s1, lax.ppermute(jnp.stack([s0, s1]), "pcol", [(i, i ^ 1) for i in range(8)])


def z_sort(z, s0, s1, r3):
    even = z % 2 == 0
    return [
        jnp.where(even, s0, r3[0]),
        jnp.where(even, r3[0], s0),
        jnp.where(even, s1, r3[1]),
    ]


def finish_kernel(s_ref, mine, other, cmine, cother, w, b, linv, uinv, out, abuf, cbuf, lbuf):
    x, y, c, p, z = (s_ref[i] for i in range(5))

    def assemble(left, right, cleft, cright):
        for g in range(16):
            jy, jx = (y - g // 4) & 3, (x - g % 4) & 3
            rows = slice(16 * g, 16 * g + 16)
            for r in range(3):
                first, second = left[jy, jx, r], right[jx, jy, r]
                abuf[r, rows, 0:128] = first[:, 0:128]
                abuf[r, rows, 128:256] = second[:, 0:128]
                abuf[r, rows, 256:1152] = first[:, 128:1024]
                abuf[r, rows, 1152:2048] = second[:, 128:1024]
            for k in range(3):
                for i in range(2):
                    cbuf[k, i, rows, 0:128] = cleft[jy, k, i, jx]
                    cbuf[k, i, rows, 128:256] = cright[jx, k, i, jy]

    @pl.when(c == 0)
    def _():
        assemble(mine, other, cmine, cother)

    @pl.when(c == 1)
    def _():
        assemble(other, mine, cother, cmine)

    a10, a20 = cbuf[0, 0], cbuf[0, 1]
    a01, a21 = cbuf[1, 0], cbuf[1, 1]
    a02, a12 = cbuf[2, 0], cbuf[2, 1]
    u01 = mm(linv[0], a01).astype(BF)
    u02 = mm(linv[0], a02).astype(BF)
    l10 = mm(a10, uinv[0]).astype(BF)
    l20 = mm(a20, uinv[0]).astype(BF)
    u12 = mm(linv[1], (a12.astype(F32) - mm(l10, u02)).astype(BF)).astype(BF)
    l21 = mm((a21.astype(F32) - mm(l20, u01)).astype(BF), uinv[1]).astype(BF)
    l0 = mm(b[0], uinv[0]).astype(BF)
    l1 = mm((b[1].astype(F32) - mm(l0, u01)).astype(BF), uinv[1]).astype(BF)
    l2 = mm((b[2].astype(F32) - mm(l0, u02) - mm(l1, u12)).astype(BF), uinv[2]).astype(BF)
    rows = lax.broadcasted_iota(jnp.int32, (256, 256), 0)
    cols = lax.broadcasted_iota(jnp.int32, (256, 256), 1)
    minus_one = jnp.where(rows == cols, -1.0, 0.0).astype(BF)
    zero = jnp.zeros((256, 256), BF)
    m0 = pick(p, [minus_one, zero, zero, l0])
    m1 = pick(p, [zero, minus_one, zero, l1])
    m2 = pick(p, [zero, zero, minus_one, l2])
    keep = jnp.where(p < 3, 0.0, 1.0)
    lbuf[0:256, :] = l10
    lbuf[256:512, :] = l20
    lbuf[512:768, :] = m0
    lbuf[768:1024, :] = l21
    lbuf[1024:1280, :] = m1
    step = 256
    for k in range(2048 // step):
        at = slice(step * k, step * k + step)
        own = w[:, at].astype(F32)
        u0 = mm(linv[0], abuf[0, :, at]).astype(BF)
        t0 = mm(lbuf[0:768, :], u0)
        s1 = abuf[1, :, at].astype(F32) - t0[0:256]
        u1 = mm(linv[1], s1.astype(BF)).astype(BF)
        t1 = mm(lbuf[768:1280, :], u1)
        s2 = abuf[2, :, at].astype(F32) - t0[256:512] - t1[0:256]
        u2 = mm(linv[2], s2.astype(BF)).astype(BF)
        res = own * keep - t0[512:768] - t1[256:512] - mm(m2, u2)
        for i in range(step // 128):
            unit = step // 128 * k + i
            out[pl.ds(unit, 256, stride=16), :] = res[:, 128 * i : 128 * i + 128]
        if k == 0:

            @pl.when(z < 3)
            def _():
                first = slice(0, 256)
                panel = pick(z, [l0.astype(F32), l1.astype(F32), l2.astype(F32)])
                diag = pick(z, [own[:, first], s1[:, first], s2[:, first]])
                special = jnp.where(p > z, panel, jnp.where(p == z, diag, res[:, first]))
                out[pl.ds(0, 256, stride=16), :] = special[:, :128]
                out[pl.ds(1, 256, stride=16), :] = special[:, 128:]


def finish(*operands):
    return pl.pallas_call(
        finish_kernel,
        out_shape=jax.ShapeDtypeStruct((4096, 128), F32),
        in_specs=[pl.BlockSpec(memory_space=pltpu.SMEM)]
        + [pl.BlockSpec(memory_space=pltpu.VMEM)] * 8,
        out_specs=pl.BlockSpec(memory_space=pltpu.VMEM),
        scratch_shapes=[
            pltpu.VMEM((3, 256, 2048), BF),
            pltpu.VMEM((3, 2, 256, 256), BF),
            pltpu.VMEM((1280, 256), BF),
        ],
        compiler_params=pltpu.CompilerParams(vmem_limit_bytes=40 * 1024 * 1024),
    )(*operands)


def swap_cores(a):
    return lax.ppermute(a, "prow", [(i, i ^ 1) for i in range(32)])


def body(matrix, linv, uinv):
    p, z = lax.axis_index("prow"), lax.axis_index("pcol")
    y, x, c = p // 8, (p // 2) % 4, p % 2
    w = matrix.reshape(256, 2048)
    panel = w[:, :256]
    panel1 = z_far(panel, z)
    halves = jnp.stack(
        [
            jnp.concatenate([w[:, :128], w[:, 256:1152]], axis=1),
            jnp.concatenate([w[:, 128:256], w[:, 1152:]], axis=1),
        ]
    )
    parts = halves.reshape(2, 16, 16, 1024).transpose(1, 0, 2, 3).reshape(32, 16, 1024)
    piece = lax.all_to_all(parts, "prow", 0, 0)[:3]
    piece, panel1 = tie(piece, panel1)
    panel_h, panel2 = z_mid(panel, z, panel1)
    line = gather_ring(piece, 0)
    line, panel2 = tie(line, panel2)
    panel_s0, panel_s1, panel3 = z_near(z, panel_h, panel2)
    mine = gather_ring(line, 1)
    edge = line[:, :, :, :128]
    edge = jnp.stack(
        [
            jnp.where(z == 0, edge[:, 1], edge[:, 0]),
            jnp.where(z == 2, edge[:, 1], edge[:, 2]),
        ]
    )
    edge_h, edge2 = z_mid(edge, z, z_far(edge, z))
    corner = jnp.stack(z_sort(z, *z_near(z, edge_h, edge2)))
    corner, panel3 = tie(corner, panel3)
    other = swap_cores(mine)
    cmine = gather_ring(corner, 1)
    cother = swap_cores(cmine)
    b = jnp.stack(z_sort(z, panel_s0, panel_s1, panel3))
    scalars = jnp.stack([x, y, c, p, z]).astype(jnp.int32)
    out = finish(scalars, mine, other, cmine, cother, w, b, linv, uinv)
    return out.reshape(matrix.shape)


def solution(mesh):
    in_specs = (P(None, "prow", None, None, "pcol", None), P(), P())
    out_specs = P(None, "prow", None, None, "pcol", None)
    return jax.shard_map(body, mesh=mesh, in_specs=in_specs, out_specs=out_specs, check_vma=False)
```

```python
import jax
import jax.numpy as jnp
from jax import lax
from jax.experimental import pallas as pl
from jax.experimental.pallas import tpu as pltpu
from jax.sharding import PartitionSpec as P

BF = jnp.bfloat16
F32 = jnp.float32


def dev(y, x, c):
    return (y % 4) * 8 + (x % 4) * 2 + c


def mm(a, b):
    return jnp.dot(a, b, preferred_element_type=F32)


def pick(index, options):
    out = options[-1]
    for i in range(len(options) - 2, -1, -1):
        out = jnp.where(index == i, options[i], out)
    return out


def gather_ring(piece, x_core):
    got = {}
    for d in (2, 1, 3):
        pairs = []
        for y in range(4):
            for x in range(4):
                pairs.append((dev(y, x, x_core), dev(y, x + d, x_core)))
                pairs.append((dev(y, x, 1 - x_core), dev(y + d, x, 1 - x_core)))
        got[d] = lax.ppermute(piece, "prow", pairs)
    return [piece, got[1], got[2], got[3]]


def tie(*arrays):
    return lax.optimization_barrier(arrays)


def z_out(b, z):
    up = lax.ppermute(b, "pcol", [(0, 3), (1, 4), (2, 5)])
    down = lax.ppermute(b, "pcol", [(0, 5), (1, 6), (2, 7)])
    return up, down


def z_fill(b, z, up, down):
    own = jnp.where(z < 3, b, jnp.where(z < 5, up, down))
    own5 = jnp.where(z == 5, up, own)
    above = lax.ppermute(own, "pcol", [(i, (i + 1) % 8) for i in range(8)])
    below = lax.ppermute(own5, "pcol", [(i, (i - 1) % 8) for i in range(8)])
    return own, own5, above, below


def z_sort(z, own, own5, above, below):
    return [
        pick(z, [own, above, below, own, above, own, above, below]),
        pick(z, [below, own, above, below, own, above, own, above]),
        pick(z, [above, below, own, above, below, own5, below, own]),
    ]


def solve_kernel(s_ref, mine, other, cmine, cother, linv, uinv, u, small, diag, abuf, cbuf):
    x, y, c, _, z = (s_ref[i] for i in range(5))

    def assemble(bulk, corner, half):
        for j in range(4):
            for i in range(4):
                if half == 0:
                    g = 4 * ((y - j) & 3) + ((x - i) & 3)
                else:
                    g = 4 * ((y - i) & 3) + ((x - j) & 3)
                rows = pl.ds(pl.multiple_of(16 * g, 16), 16)
                for r in range(3):
                    at = 192 * j + 48 * i + 16 * r
                    part = bulk[at : at + 16, :]
                    abuf[r, rows, 128 * half : 128 * half + 128] = part[:, 0:128]
                    lane = 256 + 896 * half
                    abuf[r, rows, lane : lane + 896] = part[:, 128:1024]
                    for q in range(2):
                        at = 384 * j + 128 * r + 64 * q + 16 * i
                        cbuf[r, q, rows, 128 * half : 128 * half + 128] = corner[at : at + 16, :]

    @pl.when(c == 0)
    def _():
        assemble(mine, cmine, 0)
        assemble(other, cother, 1)

    @pl.when(c == 1)
    def _():
        assemble(other, cother, 0)
        assemble(mine, cmine, 1)

    a10, a20 = cbuf[0, 0], cbuf[0, 1]
    a01, a21 = cbuf[1, 0], cbuf[1, 1]
    a02, a12 = cbuf[2, 0], cbuf[2, 1]
    u01 = mm(linv[0], a01).astype(BF)
    u02 = mm(linv[0], a02).astype(BF)
    l10 = mm(a10, uinv[0]).astype(BF)
    l20 = mm(a20, uinv[0]).astype(BF)
    u12 = mm(linv[1], (a12.astype(F32) - mm(l10, u02)).astype(BF)).astype(BF)
    l21 = mm((a21.astype(F32) - mm(l20, u01)).astype(BF), uinv[1]).astype(BF)
    small[0], small[1], small[2] = u01, u02, u12
    u0 = mm(linv[0], abuf[0]).astype(BF)
    u[0:256, :] = u0
    s1 = abuf[1].astype(F32) - mm(l10, u0)
    u1 = mm(linv[1], s1.astype(BF)).astype(BF)
    u[256:512, :] = u1
    s2 = abuf[2].astype(F32) - mm(l20, u0) - mm(l21, u1)
    u[512:768, :] = mm(linv[2], s2.astype(BF)).astype(BF)
    diag[...] = jnp.where(z == 1, s1[:, :256], s2[:, :256])


def solve(*operands):
    return pl.pallas_call(
        solve_kernel,
        out_shape=[
            jax.ShapeDtypeStruct((768, 2048), BF),
            jax.ShapeDtypeStruct((3, 256, 256), BF),
            jax.ShapeDtypeStruct((256, 256), F32),
        ],
        in_specs=[pl.BlockSpec(memory_space=pltpu.SMEM)]
        + [pl.BlockSpec(memory_space=pltpu.VMEM)] * 6,
        out_specs=[pl.BlockSpec(memory_space=pltpu.VMEM)] * 3,
        scratch_shapes=[pltpu.VMEM((3, 256, 2048), BF), pltpu.VMEM((3, 2, 256, 256), BF)],
        compiler_params=pltpu.CompilerParams(vmem_limit_bytes=24 * 1024 * 1024),
        cost_estimate=pl.CostEstimate(
            flops=1_700_000_000, bytes_accessed=10_000_000, transcendentals=0
        ),
    )(*operands)


def finish_kernel(s_ref, u, small, diag, w, own, own5, above, below, uinv, out, lbuf):
    p, z = s_ref[3], s_ref[4]
    b0, b1, b2 = z_sort(z, own[...], own5[...], above[...], below[...])
    u01, u02, u12 = small[0], small[1], small[2]
    l0 = mm(b0, uinv[0]).astype(BF)
    l1 = mm((b1.astype(F32) - mm(l0, u01)).astype(BF), uinv[1]).astype(BF)
    l2 = mm((b2.astype(F32) - mm(l0, u02) - mm(l1, u12)).astype(BF), uinv[2]).astype(BF)
    rows = lax.broadcasted_iota(jnp.int32, (256, 256), 0)
    cols = lax.broadcasted_iota(jnp.int32, (256, 256), 1)
    minus_one = jnp.where(rows == cols, -1.0, 0.0).astype(BF)
    zero = jnp.zeros((256, 256), BF)
    lbuf[:, 0:256] = pick(p, [minus_one, zero, zero, l0])
    lbuf[:, 256:512] = pick(p, [zero, minus_one, zero, l1])
    lbuf[:, 512:768] = pick(p, [zero, zero, minus_one, l2])
    keep = jnp.where(p < 3, 0.0, 1.0)
    res = w[...].astype(F32) * keep - mm(lbuf[...], u[...])
    for k in range(16):
        out[pl.ds(k, 256, stride=16), :] = res[:, 128 * k : 128 * k + 128]

    @pl.when(z < 3)
    def _():
        panel = pick(z, [l0.astype(F32), l1.astype(F32), l2.astype(F32)])
        middle = jnp.where(z == 0, w[:, :256].astype(F32), diag[...])
        special = jnp.where(p > z, panel, jnp.where(p == z, middle, res[:, :256]))
        out[pl.ds(0, 256, stride=16), :] = special[:, :128]
        out[pl.ds(1, 256, stride=16), :] = special[:, 128:]


def finish(*operands):
    return pl.pallas_call(
        finish_kernel,
        out_shape=jax.ShapeDtypeStruct((4096, 128), F32),
        in_specs=[pl.BlockSpec(memory_space=pltpu.SMEM)]
        + [pl.BlockSpec(memory_space=pltpu.VMEM)] * 9,
        out_specs=pl.BlockSpec(memory_space=pltpu.VMEM),
        scratch_shapes=[pltpu.VMEM((256, 768), BF)],
        compiler_params=pltpu.CompilerParams(vmem_limit_bytes=24 * 1024 * 1024),
        cost_estimate=pl.CostEstimate(
            flops=900_000_000, bytes_accessed=7_000_000, transcendentals=0
        ),
    )(*operands)


def swap_cores(a):
    return lax.ppermute(a, "prow", [(i, i ^ 1) for i in range(32)])


def body(matrix, linv, uinv):
    p, z = lax.axis_index("prow"), lax.axis_index("pcol")
    y, x, c = p // 8, (p // 2) % 4, p % 2
    w = matrix.reshape(256, 2048)
    panel = w[:, :256]
    up, down = z_out(panel, z)
    halves = jnp.stack(
        [
            jnp.concatenate([w[:, :128], w[:, 256:1152]], axis=1),
            jnp.concatenate([w[:, 128:256], w[:, 1152:]], axis=1),
        ]
    )
    parts = halves.reshape(2, 16, 16, 1024).transpose(1, 0, 2, 3).reshape(32, 16, 1024)
    piece = lax.all_to_all(parts, "prow", 0, 0)[:3].reshape(48, 1024)
    piece, up, down = tie(piece, up, down)
    line = jnp.concatenate(gather_ring(piece, 0))
    blocks = [
        jnp.concatenate([line[48 * i + 16 * r : 48 * i + 16 * r + 16, :128] for i in range(4)])
        for r in range(3)
    ]
    edge = jnp.concatenate(
        [
            jnp.where(z == 0, blocks[1], blocks[0]),
            jnp.where(z == 2, blocks[1], blocks[2]),
        ]
    )
    edge_out = z_out(edge, z)
    mine = gather_ring(line, 1)
    *mine, edge_up, edge_down = tie(*mine, *edge_out)
    mine = jnp.concatenate(mine)
    other = swap_cores(mine)
    corner = jnp.concatenate(z_sort(z, *z_fill(edge, z, edge_up, edge_down)))
    corner, up, down = tie(corner, up, down)
    cmine = jnp.concatenate(gather_ring(corner, 1))
    cother = swap_cores(cmine)
    filled = z_fill(panel, z, up, down)
    scalars = jnp.stack([x, y, c, p, z]).astype(jnp.int32)
    u, small, diag = solve(scalars, mine, other, cmine, cother, linv, uinv)
    out = finish(scalars, u, small, diag, w, *filled, uinv)
    return out.reshape(matrix.shape)


def solution(mesh):
    in_specs = (P(None, "prow", None, None, "pcol", None), P(), P())
    out_specs = P(None, "prow", None, None, "pcol", None)
    return jax.shard_map(body, mesh=mesh, in_specs=in_specs, out_specs=out_specs, check_vma=False)
```

```python
import jax
import jax.numpy as jnp
from jax import lax
from jax.experimental import pallas as pl
from jax.experimental.pallas import tpu as pltpu
from jax.sharding import PartitionSpec as P

BF = jnp.bfloat16
F32 = jnp.float32


def dev(y, x, c):
    return (y % 4) * 8 + (x % 4) * 2 + c


def mm(a, b):
    return jnp.dot(a, b, preferred_element_type=F32)


def pick(index, options):
    out = options[-1]
    for i in range(len(options) - 2, -1, -1):
        out = jnp.where(index == i, options[i], out)
    return out


class Place:
    def __init__(self, index, count):
        self.index = index
        self.flags = [index == i for i in range(count)]

    def __eq__(self, other):
        return self.flags[other]


def gather_ring(piece, x_core):
    got = {}
    for d in (2, 1, 3):
        pairs = []
        for y in range(4):
            for x in range(4):
                pairs.append((dev(y, x, x_core), dev(y, x + d, x_core)))
                pairs.append((dev(y, x, 1 - x_core), dev(y + d, x, 1 - x_core)))
        got[d] = lax.ppermute(piece, "prow", pairs)
    return [piece, got[1], got[2], got[3]]


def tie(*arrays):
    return lax.optimization_barrier(arrays)


def z_out(b, z):
    up = lax.ppermute(b, "pcol", [(0, 3), (1, 4), (2, 5)])
    down = lax.ppermute(b, "pcol", [(0, 5), (1, 6), (2, 7)])
    return up, down


def z_fill(b, z, up, down):
    own = pick(z, [b, b, b, up, up, down, down, down])
    own5 = jnp.where(z == 5, up, own)
    above = lax.ppermute(own, "pcol", [(i, (i + 1) % 8) for i in range(8)])
    below = lax.ppermute(own5, "pcol", [(i, (i - 1) % 8) for i in range(8)])
    return own, own5, above, below


def z_sort(z, own, own5, above, below):
    return [
        pick(z, [own, above, below, own, above, own, above, below]),
        pick(z, [below, own, above, below, own, above, own, above]),
        pick(z, [above, below, own, above, below, own5, below, own]),
    ]


def solve_kernel(s_ref, mine, other, cmine, cother, linv, uinv, u, small, diag, abuf, cbuf):
    p, z = s_ref[0], s_ref[1]
    x, y, c = (p >> 1) & 3, p >> 3, p & 1

    def assemble(bulk, corner, half):
        for j in range(4):
            for i in range(4):
                if half == 0:
                    g = 4 * ((y - j) & 3) + ((x - i) & 3)
                else:
                    g = 4 * ((y - i) & 3) + ((x - j) & 3)
                rows = pl.ds(pl.multiple_of(16 * g, 16), 16)
                for r in range(3):
                    at = 192 * j + 48 * i + 16 * r
                    part = bulk[at : at + 16, :]
                    abuf[r, rows, 128 * half : 128 * half + 128] = part[:, 0:128]
                    lane = 256 + 896 * half
                    abuf[r, rows, lane : lane + 896] = part[:, 128:1024]
                    for q in range(2):
                        at = 384 * j + 128 * r + 64 * q + 16 * i
                        cbuf[r, q, rows, 128 * half : 128 * half + 128] = corner[at : at + 16, :]

    @pl.when(c == 0)
    def _():
        assemble(mine, cmine, 0)
        assemble(other, cother, 1)

    @pl.when(c == 1)
    def _():
        assemble(other, cother, 0)
        assemble(mine, cmine, 1)

    a10, a20 = cbuf[0, 0], cbuf[0, 1]
    a01, a21 = cbuf[1, 0], cbuf[1, 1]
    a02, a12 = cbuf[2, 0], cbuf[2, 1]
    u01 = mm(linv[0], a01).astype(BF)
    u02 = mm(linv[0], a02).astype(BF)
    l10 = mm(a10, uinv[0]).astype(BF)
    l20 = mm(a20, uinv[0]).astype(BF)
    u12 = mm(linv[1], (a12.astype(F32) - mm(l10, u02)).astype(BF)).astype(BF)
    l21 = mm((a21.astype(F32) - mm(l20, u01)).astype(BF), uinv[1]).astype(BF)
    small[0], small[1], small[2] = u01, u02, u12
    u0 = mm(linv[0], abuf[0]).astype(BF)
    u[0:256, :] = u0
    s1 = abuf[1].astype(F32) - mm(l10, u0)
    u1 = mm(linv[1], s1.astype(BF)).astype(BF)
    u[256:512, :] = u1
    s2 = abuf[2].astype(F32) - mm(l20, u0) - mm(l21, u1)
    u[512:768, :] = mm(linv[2], s2.astype(BF)).astype(BF)
    diag[...] = jnp.where(z == 1, s1[:, :256], s2[:, :256])


def solve(*operands):
    return pl.pallas_call(
        solve_kernel,
        out_shape=[
            jax.ShapeDtypeStruct((768, 2048), BF),
            jax.ShapeDtypeStruct((3, 256, 256), BF),
            jax.ShapeDtypeStruct((256, 256), F32),
        ],
        in_specs=[pl.BlockSpec(memory_space=pltpu.SMEM)]
        + [pl.BlockSpec(memory_space=pltpu.VMEM)] * 6,
        out_specs=[pl.BlockSpec(memory_space=pltpu.VMEM)] * 3,
        scratch_shapes=[pltpu.VMEM((3, 256, 2048), BF), pltpu.VMEM((3, 2, 256, 256), BF)],
        compiler_params=pltpu.CompilerParams(vmem_limit_bytes=24 * 1024 * 1024),
        cost_estimate=pl.CostEstimate(
            flops=1_700_000_000, bytes_accessed=10_000_000, transcendentals=0
        ),
    )(*operands)


def finish_kernel(s_ref, u, small, diag, w, own, own5, above, below, uinv, out, lbuf):
    p, z = s_ref[0], s_ref[1]
    b0, b1, b2 = z_sort(z, own[...], own5[...], above[...], below[...])
    u01, u02, u12 = small[0], small[1], small[2]
    l0 = mm(b0, uinv[0]).astype(BF)
    l1 = mm((b1.astype(F32) - mm(l0, u01)).astype(BF), uinv[1]).astype(BF)
    l2 = mm((b2.astype(F32) - mm(l0, u02) - mm(l1, u12)).astype(BF), uinv[2]).astype(BF)
    rows = lax.broadcasted_iota(jnp.int32, (256, 256), 0)
    cols = lax.broadcasted_iota(jnp.int32, (256, 256), 1)
    minus_one = jnp.where(rows == cols, -1.0, 0.0).astype(BF)
    zero = jnp.zeros((256, 256), BF)
    lbuf[:, 0:256] = pick(p, [minus_one, zero, zero, l0])
    lbuf[:, 256:512] = pick(p, [zero, minus_one, zero, l1])
    lbuf[:, 512:768] = pick(p, [zero, zero, minus_one, l2])
    keep = jnp.where(p < 3, 0.0, 1.0)
    res = w[...].astype(F32) * keep - mm(lbuf[...], u[...])
    for k in range(16):
        out[pl.ds(k, 256, stride=16), :] = res[:, 128 * k : 128 * k + 128]

    @pl.when(z < 3)
    def _():
        panel = pick(z, [l0.astype(F32), l1.astype(F32), l2.astype(F32)])
        middle = jnp.where(z == 0, w[:, :256].astype(F32), diag[...])
        special = jnp.where(p > z, panel, jnp.where(p == z, middle, res[:, :256]))
        out[pl.ds(0, 256, stride=16), :] = special[:, :128]
        out[pl.ds(1, 256, stride=16), :] = special[:, 128:]


def finish(*operands):
    return pl.pallas_call(
        finish_kernel,
        out_shape=jax.ShapeDtypeStruct((4096, 128), F32),
        in_specs=[pl.BlockSpec(memory_space=pltpu.SMEM)]
        + [pl.BlockSpec(memory_space=pltpu.VMEM)] * 9,
        out_specs=pl.BlockSpec(memory_space=pltpu.VMEM),
        scratch_shapes=[pltpu.VMEM((256, 768), BF)],
        compiler_params=pltpu.CompilerParams(vmem_limit_bytes=24 * 1024 * 1024),
        cost_estimate=pl.CostEstimate(
            flops=900_000_000, bytes_accessed=7_000_000, transcendentals=0
        ),
    )(*operands)


def swap_cores(a):
    return lax.ppermute(a, "prow", [(i, i ^ 1) for i in range(32)])


def body(matrix, linv, uinv):
    p, z = lax.axis_index("prow"), lax.axis_index("pcol")
    scalars = jnp.stack([p, z]).astype(jnp.int32)
    z = Place(z, 8)
    matrix, scalars, *z.flags = tie(matrix, scalars, *z.flags)
    w = matrix.reshape(256, 2048)
    panel = w[:, :256]
    up, down = z_out(panel, z)
    halves = jnp.stack(
        [
            jnp.concatenate([w[:, :128], w[:, 256:1152]], axis=1),
            jnp.concatenate([w[:, 128:256], w[:, 1152:]], axis=1),
        ]
    )
    parts = halves.reshape(2, 16, 16, 1024).transpose(1, 0, 2, 3).reshape(32, 16, 1024)
    piece = lax.all_to_all(parts, "prow", 0, 0)[:3].reshape(48, 1024)
    piece, up, down = tie(piece, up, down)
    line = jnp.concatenate(gather_ring(piece, 0))
    blocks = [
        jnp.concatenate([line[48 * i + 16 * r : 48 * i + 16 * r + 16, :128] for i in range(4)])
        for r in range(3)
    ]
    edge = jnp.concatenate(
        [
            jnp.where(z == 0, blocks[1], blocks[0]),
            jnp.where(z == 2, blocks[1], blocks[2]),
        ]
    )
    edge_out = z_out(edge, z)
    mine = gather_ring(line, 1)
    *mine, edge_up, edge_down = tie(*mine, *edge_out)
    mine = jnp.concatenate(mine)
    other = swap_cores(mine)
    corner = jnp.concatenate(z_sort(z, *z_fill(edge, z, edge_up, edge_down)))
    corner, up, down = tie(corner, up, down)
    cmine = jnp.concatenate(gather_ring(corner, 1))
    cother = swap_cores(cmine)
    filled = z_fill(panel, z, up, down)
    u, small, diag = solve(scalars, mine, other, cmine, cother, linv, uinv)
    out = finish(scalars, u, small, diag, w, *filled, uinv)
    return out.reshape(matrix.shape)


def solution(mesh):
    in_specs = (P(None, "prow", None, None, "pcol", None), P(), P())
    out_specs = P(None, "prow", None, None, "pcol", None)
    return jax.shard_map(body, mesh=mesh, in_specs=in_specs, out_specs=out_specs, check_vma=False)
```

```python
import jax
import jax.numpy as jnp
from jax import lax
from jax.experimental import pallas as pl
from jax.experimental.pallas import tpu as pltpu
from jax.sharding import PartitionSpec as P

BF = jnp.bfloat16
F32 = jnp.float32


def dev(y, x, c):
    return (y % 4) * 8 + (x % 4) * 2 + c


def mm(a, b):
    return jnp.dot(a, b, preferred_element_type=F32)


def pick(index, options):
    out = options[-1]
    for i in range(len(options) - 2, -1, -1):
        out = jnp.where(index == i, options[i], out)
    return out


class Place:
    def __init__(self, index, count):
        self.index = index
        self.flags = [index == i for i in range(count)]

    def __eq__(self, other):
        return self.flags[other]


def gather_ring(piece, x_core):
    got = {}
    for d in (2, 1, 3):
        pairs = []
        for y in range(4):
            for x in range(4):
                pairs.append((dev(y, x, x_core), dev(y, x + d, x_core)))
                pairs.append((dev(y, x, 1 - x_core), dev(y + d, x, 1 - x_core)))
        got[d] = lax.ppermute(piece, "prow", pairs)
    return [piece, got[1], got[2], got[3]]


def tie(*arrays):
    return lax.optimization_barrier(arrays)


def z_out(b, z):
    up = lax.ppermute(b, "pcol", [(0, 3), (1, 4), (2, 5)])
    down = lax.ppermute(b, "pcol", [(0, 6), (1, 7), (2, 0)])
    return up, down


def z_fill(b, z, up, down):
    own = pick(z, [b, b, b, up, up, up, down, down])
    second = jnp.where(z == 0, down, own)
    above = lax.ppermute(own, "pcol", [(i, (i + 1) % 8) for i in range(8)])
    below = lax.ppermute(second, "pcol", [(i, (i - 1) % 8) for i in range(8)])
    return own, second, above, below


def z_sort(z, own, second, above, below):
    return [
        pick(z, [own, above, below, own, above, below, own, above]),
        pick(z, [below, own, above, below, own, above, below, own]),
        pick(z, [second, below, own, above, below, own, above, below]),
    ]


def solve_kernel(s_ref, mine, other, cmine, cother, linv, uinv, u, small, diag, abuf, cbuf):
    p, z = s_ref[0], s_ref[1]
    x, y, c = (p >> 1) & 3, p >> 3, p & 1

    def assemble(bulk, corner, half):
        for j in range(4):
            for i in range(4):
                if half == 0:
                    g = 4 * ((y - j) & 3) + ((x - i) & 3)
                else:
                    g = 4 * ((y - i) & 3) + ((x - j) & 3)
                rows = pl.ds(pl.multiple_of(16 * g, 16), 16)
                for r in range(3):
                    at = 192 * j + 48 * i + 16 * r
                    part = bulk[at : at + 16, :]
                    abuf[r, rows, 128 * half : 128 * half + 128] = part[:, 0:128]
                    lane = 256 + 896 * half
                    abuf[r, rows, lane : lane + 896] = part[:, 128:1024]
                    for q in range(2):
                        at = 384 * j + 128 * r + 64 * q + 16 * i
                        cbuf[r, q, rows, 128 * half : 128 * half + 128] = corner[at : at + 16, :]

    @pl.when(c == 0)
    def _():
        assemble(mine, cmine, 0)
        assemble(other, cother, 1)

    @pl.when(c == 1)
    def _():
        assemble(other, cother, 0)
        assemble(mine, cmine, 1)

    a10, a20 = cbuf[0, 0], cbuf[0, 1]
    a01, a21 = cbuf[1, 0], cbuf[1, 1]
    a02, a12 = cbuf[2, 0], cbuf[2, 1]
    u01 = mm(linv[0], a01).astype(BF)
    u02 = mm(linv[0], a02).astype(BF)
    l10 = mm(a10, uinv[0]).astype(BF)
    l20 = mm(a20, uinv[0]).astype(BF)
    u12 = mm(linv[1], (a12.astype(F32) - mm(l10, u02)).astype(BF)).astype(BF)
    l21 = mm((a21.astype(F32) - mm(l20, u01)).astype(BF), uinv[1]).astype(BF)
    small[0], small[1], small[2] = u01, u02, u12
    u0 = mm(linv[0], abuf[0]).astype(BF)
    u[0:256, :] = u0
    s1 = abuf[1].astype(F32) - mm(l10, u0)
    u1 = mm(linv[1], s1.astype(BF)).astype(BF)
    u[256:512, :] = u1
    s2 = abuf[2].astype(F32) - mm(l20, u0) - mm(l21, u1)
    u[512:768, :] = mm(linv[2], s2.astype(BF)).astype(BF)
    diag[...] = jnp.where(z == 1, s1[:, :256], s2[:, :256])


def solve(*operands):
    return pl.pallas_call(
        solve_kernel,
        out_shape=[
            jax.ShapeDtypeStruct((768, 2048), BF),
            jax.ShapeDtypeStruct((3, 256, 256), BF),
            jax.ShapeDtypeStruct((256, 256), F32),
        ],
        in_specs=[pl.BlockSpec(memory_space=pltpu.SMEM)]
        + [pl.BlockSpec(memory_space=pltpu.VMEM)] * 6,
        out_specs=[pl.BlockSpec(memory_space=pltpu.VMEM)] * 3,
        scratch_shapes=[pltpu.VMEM((3, 256, 2048), BF), pltpu.VMEM((3, 2, 256, 256), BF)],
        compiler_params=pltpu.CompilerParams(vmem_limit_bytes=24 * 1024 * 1024),
        cost_estimate=pl.CostEstimate(
            flops=1_700_000_000, bytes_accessed=10_000_000, transcendentals=0
        ),
    )(*operands)


def finish_kernel(s_ref, u, small, diag, w, own, own5, above, below, uinv, out, lbuf):
    p, z = s_ref[0], s_ref[1]
    b0, b1, b2 = z_sort(z, own[...], own5[...], above[...], below[...])
    u01, u02, u12 = small[0], small[1], small[2]
    l0 = mm(b0, uinv[0]).astype(BF)
    l1 = mm((b1.astype(F32) - mm(l0, u01)).astype(BF), uinv[1]).astype(BF)
    l2 = mm((b2.astype(F32) - mm(l0, u02) - mm(l1, u12)).astype(BF), uinv[2]).astype(BF)
    rows = lax.broadcasted_iota(jnp.int32, (256, 256), 0)
    cols = lax.broadcasted_iota(jnp.int32, (256, 256), 1)
    minus_one = jnp.where(rows == cols, -1.0, 0.0).astype(BF)
    zero = jnp.zeros((256, 256), BF)
    lbuf[:, 0:256] = pick(p, [minus_one, zero, zero, l0])
    lbuf[:, 256:512] = pick(p, [zero, minus_one, zero, l1])
    lbuf[:, 512:768] = pick(p, [zero, zero, minus_one, l2])
    keep = jnp.where(p < 3, 0.0, 1.0)
    res = w[...].astype(F32) * keep - mm(lbuf[...], u[...])
    for k in range(16):
        out[pl.ds(k, 256, stride=16), :] = res[:, 128 * k : 128 * k + 128]

    @pl.when(z < 3)
    def _():
        panel = pick(z, [l0.astype(F32), l1.astype(F32), l2.astype(F32)])
        middle = jnp.where(z == 0, w[:, :256].astype(F32), diag[...])
        special = jnp.where(p > z, panel, jnp.where(p == z, middle, res[:, :256]))
        out[pl.ds(0, 256, stride=16), :] = special[:, :128]
        out[pl.ds(1, 256, stride=16), :] = special[:, 128:]


def finish(*operands):
    return pl.pallas_call(
        finish_kernel,
        out_shape=jax.ShapeDtypeStruct((4096, 128), F32),
        in_specs=[pl.BlockSpec(memory_space=pltpu.SMEM)]
        + [pl.BlockSpec(memory_space=pltpu.VMEM)] * 9,
        out_specs=pl.BlockSpec(memory_space=pltpu.VMEM),
        scratch_shapes=[pltpu.VMEM((256, 768), BF)],
        compiler_params=pltpu.CompilerParams(vmem_limit_bytes=24 * 1024 * 1024),
        cost_estimate=pl.CostEstimate(
            flops=900_000_000, bytes_accessed=7_000_000, transcendentals=0
        ),
    )(*operands)


def swap_cores(a):
    return lax.ppermute(a, "prow", [(i, i ^ 1) for i in range(32)])


def body(matrix, linv, uinv):
    p, z = lax.axis_index("prow"), lax.axis_index("pcol")
    scalars = jnp.stack([p, z]).astype(jnp.int32)
    z = Place(z, 8)
    matrix, scalars, *z.flags = tie(matrix, scalars, *z.flags)
    w = matrix.reshape(256, 2048)
    panel = w[:, :256]
    up, down = z_out(panel, z)
    halves = jnp.stack(
        [
            jnp.concatenate([w[:, :128], w[:, 256:1152]], axis=1),
            jnp.concatenate([w[:, 128:256], w[:, 1152:]], axis=1),
        ]
    )
    parts = halves.reshape(2, 16, 16, 1024).transpose(1, 0, 2, 3).reshape(32, 16, 1024)
    piece = lax.all_to_all(parts, "prow", 0, 0)[:3].reshape(48, 1024)
    piece, up, down = tie(piece, up, down)
    line = jnp.concatenate(gather_ring(piece, 0))
    blocks = [
        jnp.concatenate([line[48 * i + 16 * r : 48 * i + 16 * r + 16, :128] for i in range(4)])
        for r in range(3)
    ]
    edge = jnp.concatenate(
        [
            jnp.where(z == 0, blocks[1], blocks[0]),
            jnp.where(z == 2, blocks[1], blocks[2]),
        ]
    )
    edge_out = z_out(edge, z)
    mine = gather_ring(line, 1)
    *mine, edge_up, edge_down = tie(*mine, *edge_out)
    mine = jnp.concatenate(mine)
    other = swap_cores(mine)
    corner = jnp.concatenate(z_sort(z, *z_fill(edge, z, edge_up, edge_down)))
    cmine = gather_ring(corner, 1)
    cmine[2], up, down = tie(cmine[2], up, down)
    filled = z_fill(panel, z, up, down)
    cother = swap_cores(jnp.concatenate(cmine))
    cmine = jnp.concatenate(cmine)
    u, small, diag = solve(scalars, mine, other, cmine, cother, linv, uinv)
    out = finish(scalars, u, small, diag, w, *filled, uinv)
    return out.reshape(matrix.shape)


def solution(mesh):
    in_specs = (P(None, "prow", None, None, "pcol", None), P(), P())
    out_specs = P(None, "prow", None, None, "pcol", None)
    return jax.shard_map(body, mesh=mesh, in_specs=in_specs, out_specs=out_specs, check_vma=False)
```

```python
import jax
import jax.numpy as jnp
from jax import lax
from jax.experimental import pallas as pl
from jax.experimental.pallas import tpu as pltpu
from jax.sharding import PartitionSpec as P

BF = jnp.bfloat16
F32 = jnp.float32


def dev(y, x, c):
    return (y % 4) * 8 + (x % 4) * 2 + c


def mm(a, b):
    return jnp.dot(a, b, preferred_element_type=F32)


def pick(index, options):
    out = options[-1]
    for i in range(len(options) - 2, -1, -1):
        out = jnp.where(index == i, options[i], out)
    return out


class Place:
    def __init__(self, index, count):
        self.index = index
        self.flags = [index == i for i in range(count)]

    def __eq__(self, other):
        return self.flags[other]


def gather_ring(piece, x_core, order=(2, 1, 3)):
    got = {}
    for d in order:
        pairs = []
        for y in range(4):
            for x in range(4):
                pairs.append((dev(y, x, x_core), dev(y, x + d, x_core)))
                pairs.append((dev(y, x, 1 - x_core), dev(y + d, x, 1 - x_core)))
        got[d] = lax.ppermute(piece, "prow", pairs)
    return [piece, got[1], got[2], got[3]]


def tie(*arrays):
    return lax.optimization_barrier(arrays)


def z_out(b, z):
    up = lax.ppermute(b, "pcol", [(0, 3), (1, 4), (2, 5)])
    down = lax.ppermute(b, "pcol", [(0, 6), (1, 7), (2, 0)])
    return up, down


def z_fill(b, z, up, down):
    own = pick(z, [b, b, b, up, up, up, down, down])
    second = jnp.where(z == 0, down, own)
    above = lax.ppermute(own, "pcol", [(i, (i + 1) % 8) for i in range(8)])
    below = lax.ppermute(second, "pcol", [(i, (i - 1) % 8) for i in range(8)])
    return own, second, above, below


def z_sort(z, own, second, above, below):
    return [
        pick(z, [own, above, below, own, above, below, own, above]),
        pick(z, [below, own, above, below, own, above, below, own]),
        pick(z, [second, below, own, above, below, own, above, below]),
    ]


def solve_kernel(s_ref, mine, other, cmine, cother, linv, uinv, u, small, diag, abuf, cbuf):
    p, z = s_ref[0], s_ref[1]
    x, y, c = (p >> 1) & 3, p >> 3, p & 1

    def assemble(bulk, corner, half):
        for j in range(4):
            for i in range(4):
                if half == 0:
                    g = 4 * ((y - j) & 3) + ((x - i) & 3)
                else:
                    g = 4 * ((y - i) & 3) + ((x - j) & 3)
                rows = pl.ds(pl.multiple_of(16 * g, 16), 16)
                for r in range(3):
                    at = 192 * j + 48 * i + 16 * r
                    part = bulk[at : at + 16, :]
                    for k in range(8):
                        lane = 256 * k + 128 * half
                        abuf[r, rows, lane : lane + 128] = part[:, 128 * k : 128 * k + 128]
                    for q in range(2):
                        at = 384 * j + 128 * r + 64 * q + 16 * i
                        cbuf[r, q, rows, 128 * half : 128 * half + 128] = corner[at : at + 16, :]

    @pl.when(c == 0)
    def _():
        assemble(mine, cmine, 0)
        assemble(other, cother, 1)

    @pl.when(c == 1)
    def _():
        assemble(other, cother, 0)
        assemble(mine, cmine, 1)

    a10, a20 = cbuf[0, 0], cbuf[0, 1]
    a01, a21 = cbuf[1, 0], cbuf[1, 1]
    a02, a12 = cbuf[2, 0], cbuf[2, 1]
    u01 = mm(linv[0], a01).astype(BF)
    u02 = mm(linv[0], a02).astype(BF)
    l10 = mm(a10, uinv[0]).astype(BF)
    l20 = mm(a20, uinv[0]).astype(BF)
    u12 = mm(linv[1], (a12.astype(F32) - mm(l10, u02)).astype(BF)).astype(BF)
    l21 = mm((a21.astype(F32) - mm(l20, u01)).astype(BF), uinv[1]).astype(BF)
    small[0], small[1], small[2] = u01, u02, u12
    u0 = mm(linv[0], abuf[0]).astype(BF)
    u[0:256, :] = u0
    s1 = abuf[1].astype(F32) - mm(l10, u0)
    u1 = mm(linv[1], s1.astype(BF)).astype(BF)
    u[256:512, :] = u1
    s2 = abuf[2].astype(F32) - mm(l20, u0) - mm(l21, u1)
    u[512:768, :] = mm(linv[2], s2.astype(BF)).astype(BF)
    diag[...] = jnp.where(z == 1, s1[:, :256], s2[:, :256])


def solve(*operands):
    return pl.pallas_call(
        solve_kernel,
        out_shape=[
            jax.ShapeDtypeStruct((768, 2048), BF),
            jax.ShapeDtypeStruct((3, 256, 256), BF),
            jax.ShapeDtypeStruct((256, 256), F32),
        ],
        in_specs=[pl.BlockSpec(memory_space=pltpu.SMEM)]
        + [pl.BlockSpec(memory_space=pltpu.VMEM)] * 6,
        out_specs=[pl.BlockSpec(memory_space=pltpu.VMEM)] * 3,
        scratch_shapes=[pltpu.VMEM((3, 256, 2048), BF), pltpu.VMEM((3, 2, 256, 256), BF)],
        compiler_params=pltpu.CompilerParams(vmem_limit_bytes=24 * 1024 * 1024),
        cost_estimate=pl.CostEstimate(
            flops=1_700_000_000, bytes_accessed=10_000_000, transcendentals=0
        ),
    )(*operands)


def finish_kernel(s_ref, u, small, diag, w, own, own5, above, below, uinv, out, lbuf):
    p, z = s_ref[0], s_ref[1]
    b0, b1, b2 = z_sort(z, own[...], own5[...], above[...], below[...])
    u01, u02, u12 = small[0], small[1], small[2]
    l0 = mm(b0, uinv[0]).astype(BF)
    l1 = mm((b1.astype(F32) - mm(l0, u01)).astype(BF), uinv[1]).astype(BF)
    l2 = mm((b2.astype(F32) - mm(l0, u02) - mm(l1, u12)).astype(BF), uinv[2]).astype(BF)
    rows = lax.broadcasted_iota(jnp.int32, (256, 256), 0)
    cols = lax.broadcasted_iota(jnp.int32, (256, 256), 1)
    minus_one = jnp.where(rows == cols, -1.0, 0.0).astype(BF)
    zero = jnp.zeros((256, 256), BF)
    lbuf[:, 0:256] = pick(p, [minus_one, zero, zero, l0])
    lbuf[:, 256:512] = pick(p, [zero, minus_one, zero, l1])
    lbuf[:, 512:768] = pick(p, [zero, zero, minus_one, l2])
    keep = jnp.where(p < 3, 0.0, 1.0)
    res = w[...].astype(F32) * keep - mm(lbuf[...], u[...])
    for k in range(16):
        out[pl.ds(k, 256, stride=16), :] = res[:, 128 * k : 128 * k + 128]

    @pl.when(z < 3)
    def _():
        panel = pick(z, [l0.astype(F32), l1.astype(F32), l2.astype(F32)])
        middle = jnp.where(z == 0, w[:, :256].astype(F32), diag[...])
        special = jnp.where(p > z, panel, jnp.where(p == z, middle, res[:, :256]))
        out[pl.ds(0, 256, stride=16), :] = special[:, :128]
        out[pl.ds(1, 256, stride=16), :] = special[:, 128:]


def finish(*operands):
    return pl.pallas_call(
        finish_kernel,
        out_shape=jax.ShapeDtypeStruct((4096, 128), F32),
        in_specs=[pl.BlockSpec(memory_space=pltpu.SMEM)]
        + [pl.BlockSpec(memory_space=pltpu.VMEM)] * 9,
        out_specs=pl.BlockSpec(memory_space=pltpu.VMEM),
        scratch_shapes=[pltpu.VMEM((256, 768), BF)],
        compiler_params=pltpu.CompilerParams(vmem_limit_bytes=24 * 1024 * 1024),
        cost_estimate=pl.CostEstimate(
            flops=900_000_000, bytes_accessed=7_000_000, transcendentals=0
        ),
    )(*operands)


def swap_cores(a):
    return lax.ppermute(a, "prow", [(i, i ^ 1) for i in range(32)])


def body(matrix, linv, uinv):
    p, z = lax.axis_index("prow"), lax.axis_index("pcol")
    scalars = jnp.stack([p, z]).astype(jnp.int32)
    z = Place(z, 8)
    matrix, scalars, *z.flags = tie(matrix, scalars, *z.flags)
    w = matrix.reshape(256, 2048)
    panel = w[:, :256]
    up, down = z_out(panel, z)
    parts = matrix.reshape(16, 16, 8, 2, 128).transpose(0, 3, 1, 2, 4)
    parts = parts.reshape(32, 16, 8, 128)
    piece = lax.all_to_all(parts, "prow", 0, 0)[:3].reshape(48, 1024)
    piece, up, down = tie(piece, up, down)
    line = jnp.concatenate(gather_ring(piece, 0))
    blocks = [
        jnp.concatenate([line[48 * i + 16 * r : 48 * i + 16 * r + 16, :128] for i in range(4)])
        for r in range(3)
    ]
    edge = jnp.concatenate(
        [
            jnp.where(z == 0, blocks[1], blocks[0]),
            jnp.where(z == 2, blocks[1], blocks[2]),
        ]
    )
    edge_out = z_out(edge, z)
    mine = gather_ring(line, 1, (1, 3, 2))
    *mine, edge_up, edge_down = tie(*mine, *edge_out)
    mine = jnp.concatenate(mine)
    other = swap_cores(mine)
    corner = jnp.concatenate(z_sort(z, *z_fill(edge, z, edge_up, edge_down)))
    cmine = gather_ring(corner, 1)
    cmine[2], up, down = tie(cmine[2], up, down)
    filled = z_fill(panel, z, up, down)
    cother = swap_cores(jnp.concatenate(cmine))
    cmine = jnp.concatenate(cmine)
    u, small, diag = solve(scalars, mine, other, cmine, cother, linv, uinv)
    out = finish(scalars, u, small, diag, w, *filled, uinv)
    return out.reshape(matrix.shape)


def solution(mesh):
    in_specs = (P(None, "prow", None, None, "pcol", None), P(), P())
    out_specs = P(None, "prow", None, None, "pcol", None)
    return jax.shard_map(body, mesh=mesh, in_specs=in_specs, out_specs=out_specs, check_vma=False)
```

```python
import jax
import jax.numpy as jnp
from jax import lax
from jax.experimental import pallas as pl
from jax.experimental.pallas import tpu as pltpu
from jax.sharding import PartitionSpec as P

BF = jnp.bfloat16
F32 = jnp.float32


def dev(y, x, c):
    return (y % 4) * 8 + (x % 4) * 2 + c


def mm(a, b):
    return jnp.dot(a, b, preferred_element_type=F32)


def pick(index, options):
    out = options[-1]
    for i in range(len(options) - 2, -1, -1):
        out = jnp.where(index == i, options[i], out)
    return out


class Place:
    def __init__(self, index, count):
        self.index = index
        self.flags = [index == i for i in range(count)]

    def __eq__(self, other):
        return self.flags[other]


def gather_ring(piece, x_core, order=(1, 3, 2)):
    got = {}
    for d in order:
        pairs = []
        for y in range(4):
            for x in range(4):
                pairs.append((dev(y, x, x_core), dev(y, x + d, x_core)))
                pairs.append((dev(y, x, 1 - x_core), dev(y + d, x, 1 - x_core)))
        got[d] = lax.ppermute(piece, "prow", pairs)
    return [piece, got[1], got[2], got[3]]


def tie(*arrays):
    return lax.optimization_barrier(arrays)


def z_out(b, z):
    up = lax.ppermute(b, "pcol", [(0, 3), (1, 4), (2, 5)])
    down = lax.ppermute(b, "pcol", [(0, 6), (1, 7), (2, 0)])
    return up, down


def z_fill(b, z, up, down):
    own = pick(z, [b, b, b, up, up, up, down, down])
    second = jnp.where(z == 0, down, own)
    above = lax.ppermute(own, "pcol", [(i, (i + 1) % 8) for i in range(8)])
    below = lax.ppermute(second, "pcol", [(i, (i - 1) % 8) for i in range(8)])
    return own, second, above, below


def z_sort(z, own, second, above, below):
    return [
        pick(z, [own, above, below, own, above, below, own, above]),
        pick(z, [below, own, above, below, own, above, below, own]),
        pick(z, [second, below, own, above, below, own, above, below]),
    ]


def solve_kernel(s_ref, mine, other, cmine, cother, linv, uinv, u, small, diag, abuf, cbuf):
    p, z = s_ref[0], s_ref[1]
    x, y, c = (p >> 1) & 3, p >> 3, p & 1

    def assemble(bulk, corner, half):
        for j in range(4):
            for i in range(4):
                if half == 0:
                    g = 4 * ((y - j) & 3) + ((x - i) & 3)
                else:
                    g = 4 * ((y - i) & 3) + ((x - j) & 3)
                rows = pl.ds(pl.multiple_of(16 * g, 16), 16)
                for r in range(3):
                    at = 192 * j + 48 * i + 16 * r
                    part = bulk[at : at + 16, :]
                    for k in range(8):
                        lane = 256 * k + 128 * half
                        abuf[r, rows, lane : lane + 128] = part[:, 128 * k : 128 * k + 128]
                    for q in range(2):
                        at = 384 * j + 128 * r + 64 * q + 16 * i
                        cbuf[r, q, rows, 128 * half : 128 * half + 128] = corner[at : at + 16, :]

    @pl.when(c == 0)
    def _():
        assemble(mine, cmine, 0)
        assemble(other, cother, 1)

    @pl.when(c == 1)
    def _():
        assemble(other, cother, 0)
        assemble(mine, cmine, 1)

    a10, a20 = cbuf[0, 0], cbuf[0, 1]
    a01, a21 = cbuf[1, 0], cbuf[1, 1]
    a02, a12 = cbuf[2, 0], cbuf[2, 1]
    u01 = mm(linv[0], a01).astype(BF)
    u02 = mm(linv[0], a02).astype(BF)
    l10 = mm(a10, uinv[0]).astype(BF)
    l20 = mm(a20, uinv[0]).astype(BF)
    u12 = mm(linv[1], (a12.astype(F32) - mm(l10, u02)).astype(BF)).astype(BF)
    l21 = mm((a21.astype(F32) - mm(l20, u01)).astype(BF), uinv[1]).astype(BF)
    small[0], small[1], small[2] = u01, u02, u12
    u0 = mm(linv[0], abuf[0]).astype(BF)
    u[0:256, :] = u0
    s1 = abuf[1].astype(F32) - mm(l10, u0)
    u1 = mm(linv[1], s1.astype(BF)).astype(BF)
    u[256:512, :] = u1
    s2 = abuf[2].astype(F32) - mm(l20, u0) - mm(l21, u1)
    u[512:768, :] = mm(linv[2], s2.astype(BF)).astype(BF)
    diag[...] = jnp.where(z == 1, s1[:, :256], s2[:, :256])


def solve(*operands):
    return pl.pallas_call(
        solve_kernel,
        out_shape=[
            jax.ShapeDtypeStruct((768, 2048), BF),
            jax.ShapeDtypeStruct((3, 256, 256), BF),
            jax.ShapeDtypeStruct((256, 256), F32),
        ],
        in_specs=[pl.BlockSpec(memory_space=pltpu.SMEM)]
        + [pl.BlockSpec(memory_space=pltpu.VMEM)] * 6,
        out_specs=[pl.BlockSpec(memory_space=pltpu.VMEM)] * 3,
        scratch_shapes=[pltpu.VMEM((3, 256, 2048), BF), pltpu.VMEM((3, 2, 256, 256), BF)],
        compiler_params=pltpu.CompilerParams(vmem_limit_bytes=24 * 1024 * 1024),
        cost_estimate=pl.CostEstimate(
            flops=1_700_000_000, bytes_accessed=10_000_000, transcendentals=0
        ),
    )(*operands)


def finish_kernel(s_ref, u, small, diag, w, own, own5, above, below, uinv, out, lbuf):
    p, z = s_ref[0], s_ref[1]
    b0, b1, b2 = z_sort(z, own[...], own5[...], above[...], below[...])
    u01, u02, u12 = small[0], small[1], small[2]
    l0 = mm(b0, uinv[0]).astype(BF)
    l1 = mm((b1.astype(F32) - mm(l0, u01)).astype(BF), uinv[1]).astype(BF)
    l2 = mm((b2.astype(F32) - mm(l0, u02) - mm(l1, u12)).astype(BF), uinv[2]).astype(BF)
    rows = lax.broadcasted_iota(jnp.int32, (256, 256), 0)
    cols = lax.broadcasted_iota(jnp.int32, (256, 256), 1)
    minus_one = jnp.where(rows == cols, -1.0, 0.0).astype(BF)
    zero = jnp.zeros((256, 256), BF)
    lbuf[:, 0:256] = pick(p, [minus_one, zero, zero, l0])
    lbuf[:, 256:512] = pick(p, [zero, minus_one, zero, l1])
    lbuf[:, 512:768] = pick(p, [zero, zero, minus_one, l2])
    keep = jnp.where(p < 3, 0.0, 1.0)
    res = w[...].astype(F32) * keep - mm(lbuf[...], u[...])
    for k in range(16):
        out[pl.ds(k, 256, stride=16), :] = res[:, 128 * k : 128 * k + 128]

    @pl.when(z < 3)
    def _():
        panel = pick(z, [l0.astype(F32), l1.astype(F32), l2.astype(F32)])
        middle = jnp.where(z == 0, w[:, :256].astype(F32), diag[...])
        special = jnp.where(p > z, panel, jnp.where(p == z, middle, res[:, :256]))
        out[pl.ds(0, 256, stride=16), :] = special[:, :128]
        out[pl.ds(1, 256, stride=16), :] = special[:, 128:]


def finish(*operands):
    return pl.pallas_call(
        finish_kernel,
        out_shape=jax.ShapeDtypeStruct((4096, 128), F32),
        in_specs=[pl.BlockSpec(memory_space=pltpu.SMEM)]
        + [pl.BlockSpec(memory_space=pltpu.VMEM)] * 9,
        out_specs=pl.BlockSpec(memory_space=pltpu.VMEM),
        scratch_shapes=[pltpu.VMEM((256, 768), BF)],
        compiler_params=pltpu.CompilerParams(vmem_limit_bytes=24 * 1024 * 1024),
        cost_estimate=pl.CostEstimate(
            flops=900_000_000, bytes_accessed=7_000_000, transcendentals=0
        ),
    )(*operands)


def swap_cores(a):
    return lax.ppermute(a, "prow", [(i, i ^ 1) for i in range(32)])


def body(matrix, linv, uinv):
    p, z = lax.axis_index("prow"), lax.axis_index("pcol")
    scalars = jnp.stack([p, z]).astype(jnp.int32)
    z = Place(z, 8)
    matrix, scalars, *z.flags = tie(matrix, scalars, *z.flags)
    w = matrix.reshape(256, 2048)
    panel = w[:, :256]
    up, down = z_out(panel, z)
    parts = matrix.reshape(16, 16, 8, 2, 128).transpose(0, 3, 1, 2, 4)
    parts = parts.reshape(32, 16, 8, 128)
    piece = lax.all_to_all(parts, "prow", 0, 0)[:3].reshape(48, 1024)
    piece, up, down = tie(piece, up, down)
    line = jnp.concatenate(gather_ring(piece, 0))
    blocks = [
        jnp.concatenate([line[48 * i + 16 * r : 48 * i + 16 * r + 16, :128] for i in range(4)])
        for r in range(3)
    ]
    edge = jnp.concatenate(
        [
            jnp.where(z == 0, blocks[1], blocks[0]),
            jnp.where(z == 2, blocks[1], blocks[2]),
        ]
    )
    edge_out = z_out(edge, z)
    mine = gather_ring(line, 1)
    *mine, edge_up, edge_down = tie(*mine, *edge_out)
    mine = jnp.concatenate(mine)
    other = swap_cores(mine)
    corner = jnp.concatenate(z_sort(z, *z_fill(edge, z, edge_up, edge_down)))
    cmine = gather_ring(corner, 1)
    cmine[2], up, down = tie(cmine[2], up, down)
    filled = z_fill(panel, z, up, down)
    cother = swap_cores(jnp.concatenate(cmine))
    cmine = jnp.concatenate(cmine)
    u, small, diag = solve(scalars, mine, other, cmine, cother, linv, uinv)
    out = finish(scalars, u, small, diag, w, *filled, uinv)
    return out.reshape(matrix.shape)


def solution(mesh):
    in_specs = (P(None, "prow", None, None, "pcol", None), P(), P())
    out_specs = P(None, "prow", None, None, "pcol", None)
    return jax.shard_map(body, mesh=mesh, in_specs=in_specs, out_specs=out_specs, check_vma=False)
```
